32 devices in a mesh: dp: 8 (over z, core), tensor: 4 (over y, x).
Axes of the slice: x: 2, y: 2, z: 4, core: 2. Of those that a mesh axis runs over, the one named last changes fastest.
Arguments:
- x_rows: bfloat16 [256, 12288], P(('dp', 'tensor')), may hold values from -6 to 6
- block_weights: bfloat16 [1568, 128, 128], P(('dp', 'tensor')), may hold values from -0.25 to 0.25
- block_row: int32 [1568], P(('dp', 'tensor')), may hold values from 0 to 95, as said below
- block_col: int32 [1568], P(('dp', 'tensor')), may hold values from 0 to 383, as said below
- block_counts: int32 [32], P(('dp', 'tensor')), may hold values from 0 to 49, as said below
- act_grad: bfloat16 [256, 49152], P('dp', 'tensor'), may hold values from -0.75 to 0.75
Outputs:
- activation: bfloat16 [256, 49152], P('dp', 'tensor')
- grad_blocks: bfloat16 [1568, 128, 128], P(('dp', 'tensor'))
The draws below stay inside these ranges and needn't reach their ends.
Inputs may be any that keep to these rules, and one draw needn't show every extreme that they name: `block_row`: live slots of the devices with tensor index t hold, without repeats, the blocks of a butterfly pattern over the column blocks t * 96 to (t + 1) * 96 - 1: there are 96 distinct row blocks r_0 to r_(95) for t, and column block t * 96 + j has the 4 row blocks r_(j XOR o) for o in 0, 1, 2, 4. Slots that are not live hold arbitrary indices in range. `block_col`: A live slot of a device with tensor index t names a column block of t * 96 to (t + 1) * 96 - 1, and so does every other slot of that device. `block_counts`: the counts of the devices with one tensor index sum to 384; some device has 49.
All inputs are finite; a program needn't handle non-finite values.
Results may differ from the reference program's by a relative error of at most 0.014.
Values may be sent and summed in bfloat16 or wider, within the bound.
A program may use at most 64 MiB of HBM per device.

```python
import jax
import jax.numpy as jnp
from jax import lax

D = 12288
FF = 49152
BS = 128
LEVELS = 4
CB = 96
NRB = 96
CAP = 49
ROWS = 32
TOKENS = 256
SLOTS = 1568
N_DP = 8
N_TENSOR = 4


def rank_pattern(key, rank):
    keys = jax.random.split(key, 6)
    chosen = jax.random.permutation(keys[0], NRB)[:CB].astype(jnp.int32)
    column = jnp.arange(CB, dtype=jnp.int32)[:, None]
    offsets = jnp.array([0, 1, 2, 4], dtype=jnp.int32)[None, :]
    position = (column ^ offsets).reshape(-1)
    columns = (rank * CB + column + 0 * offsets).reshape(-1)
    order = jax.random.permutation(keys[1], LEVELS * CB)
    rows_all = chosen[position][order]
    cols_all = columns[order]
    share = LEVELS * CB // N_DP
    shuffle = jax.random.permutation(keys[2], N_DP)
    flags = jax.random.randint(keys[3], (N_DP // 2,), 0, 2).astype(jnp.int32)
    flags = flags.at[0].set(1)
    delta = jnp.zeros((N_DP,), jnp.int32).at[shuffle[0::2]].add(flags).at[shuffle[1::2]].add(-flags)
    counts = share + delta
    starts = jnp.cumsum(counts) - counts
    slot = jnp.arange(CAP, dtype=jnp.int32)
    source = jnp.clip(starts[:, None] + slot[None, :], 0, LEVELS * CB - 1)
    alive = slot[None, :] < counts[:, None]
    filler_rows = jax.random.randint(keys[4], (N_DP, CAP), 0, NRB).astype(jnp.int32)
    filler_cols = rank * CB + jax.random.randint(keys[5], (N_DP, CAP), 0, CB).astype(jnp.int32)
    slot_rows = jnp.where(alive, rows_all[source], filler_rows)
    slot_cols = jnp.where(alive, cols_all[source], filler_cols)
    return (slot_rows, slot_cols, counts)


def whole_pattern(key):
    base = jax.random.fold_in(key, 7)
    keys = jax.random.split(base, N_TENSOR)
    ranks = jnp.arange(N_TENSOR, dtype=jnp.int32)
    return jax.vmap(rank_pattern)(keys, ranks)


def draw_block_row(key, part):
    slot_rows, slot_cols, counts = whole_pattern(key)
    return jnp.transpose(slot_rows, (1, 0, 2)).reshape(-1).astype(jnp.int32)


def draw_block_col(key, part):
    slot_rows, slot_cols, counts = whole_pattern(key)
    return jnp.transpose(slot_cols, (1, 0, 2)).reshape(-1).astype(jnp.int32)


def draw_block_counts(key, part):
    slot_rows, slot_cols, counts = whole_pattern(key)
    return jnp.transpose(counts).reshape(-1).astype(jnp.int32)


def shard_levels(own_key, shape, pieces, least, largest):
    def one(dim, shards_of):
        heights = jax.random.uniform(jax.random.fold_in(jax.random.fold_in(own_key, 6), dim), (shards_of,), jnp.float32, least / len(pieces), largest / len(pieces))
        return jnp.repeat(jnp.exp(heights), shape[dim] // shards_of).reshape((-1,) + (1,) * (len(shape) - dim - 1))

    gain = one(*pieces[0])
    for cut in pieces[1:]:
        gain = gain * one(*cut)
    return gain


def noise(own_key, extent, scale, bound, shards=(), kind=jnp.bfloat16):
    factor_of = shard_levels(own_key, extent, shards, -0.22, 0.18) if shards else 1.0
    values = jax.random.normal(own_key, extent, jnp.float32) * scale * factor_of
    return jnp.minimum(jnp.maximum(values, -bound), bound).astype(kind)


def setup_inputs(seed: int = 0) -> dict:
    seeds = jax.random.split(jax.random.key(seed), 7)
    return {
        "x_rows": noise(seeds[0], (TOKENS, D), 1.0, 6.0, ((0, 32),)),
        "block_weights": noise(seeds[1], (SLOTS, BS, BS), (LEVELS * BS) ** -0.5, 0.25, ((0, 32),)),
        "block_row": draw_block_row(jax.random.fold_in(seeds[6], 71), 0),
        "block_col": draw_block_col(jax.random.fold_in(seeds[6], 71), 0),
        "block_counts": draw_block_counts(jax.random.fold_in(seeds[6], 71), 0),
        "act_grad": noise(seeds[5], (TOKENS, FF), (TOKENS // 4) ** -0.5, 0.75, ((0, 8), (1, 4))),
    }


def gelu_tanh(value):
    return jax.nn.gelu(value, approximate=True)

def reference(x_rows, block_weights, block_row, block_col, block_counts, act_grad):
    slots = block_weights.shape[0]
    cap = slots // (N_DP * N_TENSOR)
    within = jnp.arange(slots, dtype=jnp.int32) % cap
    live = (within < jnp.repeat(block_counts, cap)).astype(jnp.float32)
    x_three = x_rows.reshape(TOKENS, NRB, BS)
    start = jnp.zeros((TOKENS, FF // BS, BS), jnp.float32)

    def add_block(total, item):
        weight, row_block, col_block, switch = item
        picked = lax.dynamic_index_in_dim(x_three, row_block, 1, keepdims=False)
        term = jnp.dot(picked, weight, preferred_element_type=jnp.float32) * switch
        current = lax.dynamic_index_in_dim(total, col_block, 1, keepdims=False)
        return (lax.dynamic_update_index_in_dim(total, current + term, col_block, 1), None)
    pre_three, _ = lax.scan(add_block, start, (block_weights, block_row, block_col, live))
    pre = pre_three.reshape(TOKENS, FF)
    act, back = jax.vjp(gelu_tanh, pre)
    activation = act.astype(jnp.bfloat16)
    pre_grad, = back(act_grad.astype(pre.dtype))
    pre_grad = pre_grad.astype(jnp.bfloat16)
    x_four = x_rows.reshape(N_DP, ROWS, NRB, BS)
    grad_four = pre_grad.reshape(N_DP, ROWS, FF // BS, BS)

    def one_grad(item):
        row_block, col_block, switch = item
        left = lax.dynamic_index_in_dim(x_four, row_block, 2, keepdims=False).astype(jnp.float32)
        right = lax.dynamic_index_in_dim(grad_four, col_block, 2, keepdims=False).astype(jnp.float32)
        parts = jnp.einsum('dtk,dtm->dkm', left, right).astype(jnp.bfloat16)
        summed = lax.optimization_barrier(jnp.sum(parts.astype(jnp.float32), axis=0)) * switch
        return summed.astype(jnp.bfloat16)
    grad_blocks = lax.map(one_grad, (block_row, block_col, live))
    return (activation, grad_blocks)
```

```python
import functools
import math

import jax
import jax.numpy as jnp
from jax import lax
from jax.experimental import pallas as pl
from jax.experimental.pallas import tpu as pltpu
from jax.sharding import PartitionSpec as P


def gelu_tanh(value):
    return jax.nn.gelu(value, approximate=True)


def forward_kernel(row_ref, col_ref, count_ref, x_ref, w_ref, out_ref, acc_ref):
    cap, edge, _ = w_ref.shape
    blocks = acc_ref.shape[1] // edge

    @pl.loop(0, blocks)
    def _(block):
        lanes = pl.ds(pl.multiple_of(block * edge, edge), edge)
        acc_ref[:, lanes] = jnp.zeros((acc_ref.shape[0], edge), jnp.float32)

    @pl.loop(0, count_ref[0])
    def _(slot):
        source = pl.ds(pl.multiple_of(row_ref[slot] * edge, edge), edge)
        target = pl.ds(pl.multiple_of(col_ref[slot] * edge, edge), edge)
        acc_ref[:, target] += jnp.dot(
            x_ref[:, source], w_ref[slot], preferred_element_type=jnp.float32
        )

    @pl.loop(0, blocks)
    def _(block):
        lanes = pl.ds(pl.multiple_of(block * edge, edge), edge)
        out_ref[:, lanes] = acc_ref[:, lanes].astype(out_ref.dtype)


def gradient_kernel(row_ref, col_ref, count_ref, x_ref, grad_ref, out_ref):
    cap, edge, _ = out_ref.shape

    @pl.loop(0, cap)
    def _(slot):
        source = pl.ds(pl.multiple_of(row_ref[slot] * edge, edge), edge)
        target = pl.ds(pl.multiple_of(col_ref[slot] * edge, edge), edge)
        product = lax.dot_general(
            x_ref[:, source],
            grad_ref[:, target],
            (((0,), (0,)), ((), ())),
            preferred_element_type=jnp.float32,
        )
        out_ref[slot] = jnp.where(slot < count_ref[0], product, 0.0).astype(out_ref.dtype)


SMEM = pl.BlockSpec(memory_space=pltpu.SMEM)
VMEM = pl.BlockSpec(memory_space=pltpu.VMEM)
PARAMS = pltpu.CompilerParams(vmem_limit_bytes=48 * 1024 * 1024)


def move_rows(x_rows, block_weights, block_row, block_col, block_counts, act_grad):
    rank = lax.axis_index("tensor")
    cap, edge = (block_weights.shape[0], block_weights.shape[1])
    width = x_rows.shape[1]
    tokens = x_rows.shape[0] * lax.axis_size("dp") * lax.axis_size("tensor")
    local_width = act_grad.shape[1]
    col_local = block_col - rank * (local_width // edge)
    features = lax.all_gather(x_rows, ("dp", "tensor"), axis=0, tiled=True)
    partial = pl.pallas_call(
        forward_kernel,
        out_shape=jax.ShapeDtypeStruct((tokens, local_width), jnp.bfloat16),
        in_specs=[SMEM, SMEM, SMEM, VMEM, VMEM],
        out_specs=VMEM,
        scratch_shapes=[pltpu.VMEM((tokens, local_width), jnp.float32)],
        compiler_params=PARAMS,
        cost_estimate=pl.CostEstimate(
            flops=2 * cap * tokens * edge * edge,
            bytes_accessed=2 * tokens * (width + local_width) + 2 * cap * edge * edge,
            transcendentals=0,
        ),
    )(block_row, col_local, block_counts, features, block_weights)
    pre = lax.psum_scatter(partial, "dp", scatter_dimension=0, tiled=True)
    act, back = jax.vjp(gelu_tanh, pre.astype(jnp.float32))
    activation = act.astype(jnp.bfloat16)
    (pre_grad,) = back(act_grad.astype(jnp.float32))
    grads_all = lax.all_gather(pre_grad.astype(jnp.bfloat16), "dp", axis=0, tiled=True)
    grads = pl.pallas_call(
        gradient_kernel,
        out_shape=jax.ShapeDtypeStruct(block_weights.shape, jnp.bfloat16),
        in_specs=[SMEM, SMEM, SMEM, VMEM, VMEM],
        out_specs=VMEM,
        compiler_params=PARAMS,
        cost_estimate=pl.CostEstimate(
            flops=2 * cap * tokens * edge * edge,
            bytes_accessed=2 * tokens * (width + local_width) + 2 * cap * edge * edge,
            transcendentals=0,
        ),
    )(block_row, col_local, block_counts, features, grads_all)
    return (activation, grads)


def move_weights(x_rows, block_weights, block_row, block_col, block_counts, act_grad):
    rank = lax.axis_index("tensor")
    n_data = lax.axis_size("dp")
    cap, edge = (block_weights.shape[0], block_weights.shape[1])
    tok_rows, width = x_rows.shape
    row_blocks = width // edge
    rows, local_width = act_grad.shape
    col_blocks = local_width // edge
    slot_ids = jnp.arange(cap, dtype=jnp.int32)
    alive = slot_ids < block_counts[0]
    col_local = jnp.where(alive, block_col - rank * col_blocks, -1)
    gathered = lax.all_gather(x_rows, "tensor", axis=0, tiled=True)
    features = gathered.reshape(rows, row_blocks, edge)
    total_slots = n_data * cap
    start = jnp.int32(0)
    pre_three = jnp.zeros((rows, col_blocks, edge), jnp.float32)
    accumulate_all_index = jnp.zeros((total_slots,), jnp.int32)
    accumulate_all_col = jnp.zeros((total_slots,), jnp.int32)
    weights = lax.all_gather(block_weights, "dp", axis=0, tiled=True)
    indices = lax.all_gather(block_row, "dp", axis=0, tiled=True)
    targets = lax.all_gather(col_local, "dp", axis=0, tiled=True)
    count = weights.shape[0]
    group = math.gcd(count, 16)

    def one_group(acc, item):
        w_group, i_group, c_group = item
        selected = jnp.take(features, i_group, axis=1)
        product = jnp.einsum("rgk,gkm->rgm", selected, w_group, preferred_element_type=jnp.float32)
        for member in range(group):
            target = c_group[member]
            switch = (target >= 0).astype(jnp.float32)
            place = jnp.clip(target, 0, col_blocks - 1)
            current = lax.dynamic_index_in_dim(acc, place, 1, keepdims=False)
            acc = lax.dynamic_update_index_in_dim(
                acc, current + product[:, member, :] * switch, place, 1
            )
        return (acc, None)

    items = (
        weights.reshape(count // group, group, edge, edge),
        indices.reshape(count // group, group),
        targets.reshape(count // group, group),
    )
    pre_three, _ = lax.scan(one_group, pre_three, items)
    accumulate_all_index = lax.dynamic_update_slice_in_dim(accumulate_all_index, indices, start, 0)
    accumulate_all_col = lax.dynamic_update_slice_in_dim(accumulate_all_col, targets, start, 0)
    pre_three, all_index, all_col = (pre_three, accumulate_all_index, accumulate_all_col)
    pre = pre_three.reshape(rows, local_width)
    act, back = jax.vjp(gelu_tanh, pre)
    activation = act.astype(jnp.bfloat16)
    (pre_grad,) = back(act_grad.astype(jnp.float32))
    grad_three = pre_grad.astype(jnp.bfloat16).reshape(rows, col_blocks, edge)
    indices = all_index
    targets = all_col
    selected = jnp.take(features, indices, axis=1)
    switch = (targets >= 0).astype(jnp.bfloat16)
    chosen = (
        jnp.take(grad_three, jnp.clip(targets, 0, col_blocks - 1), axis=1) * switch[None, :, None]
    )
    grads = lax.psum_scatter(
        jnp.einsum("rnk,rnm->nkm", selected, chosen, preferred_element_type=jnp.float32).astype(
            jnp.bfloat16
        ),
        "dp",
        scatter_dimension=0,
        tiled=True,
    )
    return (activation, grads)


def per_device(x_rows, block_weights, block_row, block_col, block_counts, act_grad):
    row_bytes = x_rows.size * lax.axis_size("dp") * lax.axis_size("tensor")
    weight_bytes = block_weights.size * lax.axis_size("dp")
    plan = move_rows if row_bytes <= weight_bytes else move_weights
    return plan(x_rows, block_weights, block_row, block_col, block_counts, act_grad)


def solution(mesh):
    return jax.shard_map(
        per_device,
        mesh=mesh,
        in_specs=(
            P(("dp", "tensor"), None),
            P(("dp", "tensor"), None, None),
            P(("dp", "tensor")),
            P(("dp", "tensor")),
            P(("dp", "tensor")),
            P("dp", "tensor"),
        ),
        out_specs=(P("dp", "tensor"), P(("dp", "tensor"), None, None)),
        check_vma=False,
    )
```

```python
import math

import jax
import jax.numpy as jnp
from jax import lax
from jax.experimental import pallas as pl
from jax.experimental.pallas import tpu as pltpu
from jax.sharding import PartitionSpec as P


def gelu_tanh(value):
    return jax.nn.gelu(value, approximate=True)


def forward_kernel(row_ref, col_ref, count_ref, x_ref, w_ref, *rest):
    *out_refs, acc_ref = rest
    cap, edge, _ = w_ref.shape
    group = math.gcd(cap, 7)
    blocks = acc_ref.shape[1] // edge
    blocks_each = blocks // len(out_refs)

    @pl.loop(0, blocks)
    def _(block):
        lanes = pl.ds(pl.multiple_of(block * edge, edge), edge)
        acc_ref[:, lanes] = jnp.zeros((acc_ref.shape[0], edge), jnp.float32)

    @pl.loop(0, cap // group)
    def _(step):
        for member in range(group):
            slot = step * group + member
            source = pl.ds(pl.multiple_of(row_ref[slot] * edge, edge), edge)
            target = pl.ds(pl.multiple_of(col_ref[slot] * edge, edge), edge)
            product = jnp.dot(
                x_ref[:, source], w_ref[slot], preferred_element_type=jnp.float32
            )
            acc_ref[:, target] += jnp.where(slot < count_ref[0], product, 0.0)

    for part, out_ref in enumerate(out_refs):

        @pl.loop(0, blocks_each)
        def _(block):
            place = (block + part * blocks_each) * edge
            lanes = pl.ds(pl.multiple_of(block * edge, edge), edge)
            source = pl.ds(pl.multiple_of(place, edge), edge)
            out_ref[:, lanes] = acc_ref[:, source].astype(out_ref.dtype)


def gradient_kernel(row_ref, col_ref, count_ref, x_ref, *rest):
    *grad_refs, out_ref, all_ref, sems = rest
    cap, edge, _ = out_ref.shape
    group = math.gcd(cap, 7)
    each = all_ref.shape[1] // len(grad_refs)
    copies = [
        pltpu.make_async_copy(grad_ref, all_ref.at[:, pl.ds(part * each, each)], sems.at[part])
        for part, grad_ref in enumerate(grad_refs)
    ]
    for copy in copies:
        copy.start()
    for copy in copies:
        copy.wait()

    @pl.loop(0, cap // group)
    def _(step):
        for member in range(group):
            slot = step * group + member
            source = pl.ds(pl.multiple_of(row_ref[slot] * edge, edge), edge)
            target = pl.ds(pl.multiple_of(col_ref[slot] * edge, edge), edge)
            product = lax.dot_general(
                x_ref[:, source],
                all_ref[:, target],
                (((0,), (0,)), ((), ())),
                preferred_element_type=jnp.float32,
            )
            out_ref[slot] = jnp.where(slot < count_ref[0], product, 0.0).astype(out_ref.dtype)


PARTS = 2
SMEM = pl.BlockSpec(memory_space=pltpu.SMEM)
VMEM = pl.BlockSpec(memory_space=pltpu.VMEM)
PARAMS = pltpu.CompilerParams(vmem_limit_bytes=48 * 1024 * 1024)


def move_rows(x_rows, block_weights, block_row, block_col, block_counts, act_grad):
    rank = lax.axis_index("tensor")
    cap, edge = (block_weights.shape[0], block_weights.shape[1])
    width = x_rows.shape[1]
    tokens = x_rows.shape[0] * lax.axis_size("dp") * lax.axis_size("tensor")
    local_width = act_grad.shape[1]
    each = local_width // PARTS
    col_local = block_col - rank * (local_width // edge)
    features = lax.all_gather(x_rows, ("dp", "tensor"), axis=0, tiled=True)
    partial = pl.pallas_call(
        forward_kernel,
        out_shape=[jax.ShapeDtypeStruct((tokens, each), jnp.bfloat16)] * PARTS,
        in_specs=[SMEM, SMEM, SMEM, VMEM, VMEM],
        out_specs=[VMEM] * PARTS,
        scratch_shapes=[pltpu.VMEM((tokens, local_width), jnp.float32)],
        compiler_params=PARAMS,
        cost_estimate=pl.CostEstimate(
            flops=2 * cap * tokens * edge * edge,
            bytes_accessed=2 * tokens * (width + local_width) + 2 * cap * edge * edge,
            transcendentals=0,
        ),
    )(block_row, col_local, block_counts, features, block_weights)
    pre_parts = [
        lax.psum_scatter(item, "dp", scatter_dimension=0, tiled=True) for item in partial
    ]
    activations, grads_all = [], []
    ready = None
    for part, pre in enumerate(pre_parts):
        if ready is not None:
            _, pre = lax.optimization_barrier((ready, pre))
        cotangent = act_grad[:, part * each : (part + 1) * each].astype(jnp.float32)
        act, back = jax.vjp(gelu_tanh, pre.astype(jnp.float32))
        (pre_grad,) = back(cotangent)
        activations.append(act.astype(jnp.bfloat16))
        ready = pre_grad.astype(jnp.bfloat16)
        grads_all.append(lax.all_gather(ready, "dp", axis=0, tiled=True))
    activation = jnp.concatenate(activations, axis=1)
    grads = pl.pallas_call(
        gradient_kernel,
        out_shape=jax.ShapeDtypeStruct(block_weights.shape, jnp.bfloat16),
        in_specs=[SMEM, SMEM, SMEM, VMEM] + [pl.BlockSpec(memory_space=pl.ANY)] * PARTS,
        out_specs=VMEM,
        scratch_shapes=[
            pltpu.VMEM((tokens, local_width), jnp.bfloat16),
            pltpu.SemaphoreType.DMA((PARTS,)),
        ],
        compiler_params=PARAMS,
        cost_estimate=pl.CostEstimate(
            flops=2 * cap * tokens * edge * edge,
            bytes_accessed=2 * tokens * (width + local_width) + 2 * cap * edge * edge,
            transcendentals=0,
        ),
    )(block_row, col_local, block_counts, features, *grads_all)
    return (activation, grads)


def move_weights(x_rows, block_weights, block_row, block_col, block_counts, act_grad):
    rank = lax.axis_index("tensor")
    n_data = lax.axis_size("dp")
    cap, edge = (block_weights.shape[0], block_weights.shape[1])
    tok_rows, width = x_rows.shape
    row_blocks = width // edge
    rows, local_width = act_grad.shape
    col_blocks = local_width // edge
    slot_ids = jnp.arange(cap, dtype=jnp.int32)
    alive = slot_ids < block_counts[0]
    col_local = jnp.where(alive, block_col - rank * col_blocks, -1)
    gathered = lax.all_gather(x_rows, "tensor", axis=0, tiled=True)
    features = gathered.reshape(rows, row_blocks, edge)
    total_slots = n_data * cap
    start = jnp.int32(0)
    pre_three = jnp.zeros((rows, col_blocks, edge), jnp.float32)
    accumulate_all_index = jnp.zeros((total_slots,), jnp.int32)
    accumulate_all_col = jnp.zeros((total_slots,), jnp.int32)
    weights = lax.all_gather(block_weights, "dp", axis=0, tiled=True)
    indices = lax.all_gather(block_row, "dp", axis=0, tiled=True)
    targets = lax.all_gather(col_local, "dp", axis=0, tiled=True)
    count = weights.shape[0]
    group = math.gcd(count, 16)

    def one_group(acc, item):
        w_group, i_group, c_group = item
        selected = jnp.take(features, i_group, axis=1)
        product = jnp.einsum("rgk,gkm->rgm", selected, w_group, preferred_element_type=jnp.float32)
        for member in range(group):
            target = c_group[member]
            switch = (target >= 0).astype(jnp.float32)
            place = jnp.clip(target, 0, col_blocks - 1)
            current = lax.dynamic_index_in_dim(acc, place, 1, keepdims=False)
            acc = lax.dynamic_update_index_in_dim(
                acc, current + product[:, member, :] * switch, place, 1
            )
        return (acc, None)

    items = (
        weights.reshape(count // group, group, edge, edge),
        indices.reshape(count // group, group),
        targets.reshape(count // group, group),
    )
    pre_three, _ = lax.scan(one_group, pre_three, items)
    accumulate_all_index = lax.dynamic_update_slice_in_dim(accumulate_all_index, indices, start, 0)
    accumulate_all_col = lax.dynamic_update_slice_in_dim(accumulate_all_col, targets, start, 0)
    pre_three, all_index, all_col = (pre_three, accumulate_all_index, accumulate_all_col)
    pre = pre_three.reshape(rows, local_width)
    act, back = jax.vjp(gelu_tanh, pre)
    activation = act.astype(jnp.bfloat16)
    (pre_grad,) = back(act_grad.astype(jnp.float32))
    grad_three = pre_grad.astype(jnp.bfloat16).reshape(rows, col_blocks, edge)
    indices = all_index
    targets = all_col
    selected = jnp.take(features, indices, axis=1)
    switch = (targets >= 0).astype(jnp.bfloat16)
    chosen = (
        jnp.take(grad_three, jnp.clip(targets, 0, col_blocks - 1), axis=1) * switch[None, :, None]
    )
    grads = lax.psum_scatter(
        jnp.einsum("rnk,rnm->nkm", selected, chosen, preferred_element_type=jnp.float32).astype(
            jnp.bfloat16
        ),
        "dp",
        scatter_dimension=0,
        tiled=True,
    )
    return (activation, grads)


def per_device(x_rows, block_weights, block_row, block_col, block_counts, act_grad):
    row_bytes = x_rows.size * lax.axis_size("dp") * lax.axis_size("tensor")
    weight_bytes = block_weights.size * lax.axis_size("dp")
    plan = move_rows if row_bytes <= weight_bytes else move_weights
    return plan(x_rows, block_weights, block_row, block_col, block_counts, act_grad)


def solution(mesh):
    return jax.shard_map(
        per_device,
        mesh=mesh,
        in_specs=(
            P(("dp", "tensor"), None),
            P(("dp", "tensor"), None, None),
            P(("dp", "tensor")),
            P(("dp", "tensor")),
            P(("dp", "tensor")),
            P("dp", "tensor"),
        ),
        out_specs=(P("dp", "tensor"), P(("dp", "tensor"), None, None)),
        check_vma=False,
    )
```
